32 devices in a mesh: dp: 8 (over z, y), fsdp: 4 (over x, core).
Axes of the slice: x: 2, y: 2, z: 4, core: 2. Of those that a mesh axis runs over, the one named last changes fastest.
Arguments:
- tokens: bfloat16 [32768, 1024], P(('dp', 'fsdp')), may hold values from -6 to 6
- cotangent: bfloat16 [32768, 1024], P(('dp', 'fsdp')), may hold values from -6 to 6
- lengths: int32 [32, 4], P(('dp', 'fsdp')), may hold values from 0 to 1024, as said below
- attn_gain: bfloat16 [1024], P(('dp', 'fsdp')), may hold values from 0.5 to 1.5
- w_query: bfloat16 [1024, 512], P(('dp', 'fsdp')), may hold values from -0.1875 to 0.1875
- w_key: bfloat16 [1024, 512], P(('dp', 'fsdp')), may hold values from -0.1875 to 0.1875
- w_value: bfloat16 [1024, 1024], P(('dp', 'fsdp')), may hold values from -0.1875 to 0.1875
- w_outgate: bfloat16 [1024, 1024], P(('dp', 'fsdp')), may hold values from -0.1875 to 0.1875
- w_down_rank: bfloat16 [1024, 16], P(('dp', 'fsdp')), may hold values from -0.1875 to 0.1875
- w_up_rank: bfloat16 [16, 512], P(None, ('dp', 'fsdp')), may hold values from -1.5 to 1.5
- rank_bias: bfloat16 [512], P(('dp', 'fsdp')), may hold values from 0.5 to 5
- head_gain: bfloat16 [256], P(('dp', 'fsdp')), may hold values from 0.5 to 1.5
- w_output: bfloat16 [1024, 1024], P(('dp', 'fsdp')), may hold values from -0.375 to 0.375
- ffn_gain: bfloat16 [1024], P(('dp', 'fsdp')), may hold values from 0.5 to 1.5
- w_ffn_gate: bfloat16 [1024, 2816], P(('dp', 'fsdp')), may hold values from -0.1875 to 0.1875
- w_ffn_up: bfloat16 [1024, 2816], P(('dp', 'fsdp')), may hold values from -0.1875 to 0.1875
- w_ffn_down: bfloat16 [2816, 1024], P(('dp', 'fsdp')), may hold values from -0.21875 to 0.21875
Outputs:
- mixed: bfloat16 [32768, 1024], P(('dp', 'fsdp'))
- token_grad: bfloat16 [32768, 1024], P(('dp', 'fsdp'))
- grad_attn_gain: float32 [1024], P(('dp', 'fsdp'))
- grad_query: float32 [1024, 512], P(('dp', 'fsdp'))
- grad_key: float32 [1024, 512], P(('dp', 'fsdp'))
- grad_value: float32 [1024, 1024], P(('dp', 'fsdp'))
- grad_outgate: float32 [1024, 1024], P(('dp', 'fsdp'))
- grad_down_rank: float32 [1024, 16], P(('dp', 'fsdp'))
- grad_up_rank: float32 [16, 512], P(None, ('dp', 'fsdp'))
- grad_rank_bias: float32 [512], P(('dp', 'fsdp'))
- grad_head_gain: float32 [256], P(('dp', 'fsdp'))
- grad_output: float32 [1024, 1024], P(('dp', 'fsdp'))
- grad_ffn_gain: float32 [1024], P(('dp', 'fsdp'))
- grad_ffn_gate: float32 [1024, 2816], P(('dp', 'fsdp'))
- grad_ffn_up: float32 [1024, 2816], P(('dp', 'fsdp'))
- grad_ffn_down: float32 [2816, 1024], P(('dp', 'fsdp'))
The draws below stay inside these ranges and needn't reach their ends.
Inputs may be any that keep to these rules, and one draw needn't show every extreme that they name: Row i lists the lengths of device i's sequences in slot order; each entry is a multiple of 64, and 0 marks an unused entry. A row sums to between 512 and 1024; slots after the sum are padding. In every draw some device holds a single sequence of 1024 tokens.
All inputs are finite; a program needn't handle non-finite values.
Results may differ from the reference program's by a relative error of at most 0.012.
The reference program's roundings to bfloat16 on the way count: a program that leaves them out, or rounds other values in their place, can miss the bound.
Values may be sent and summed in bfloat16 or wider, within the bound.
A program may use at most 256 MiB of HBM per device.

```python
import jax
import jax.numpy as jnp
from jax import lax

D = 1024
HEADS = 4
DK = 128
DV = 256
RANK = 16
FF = 2816
GROUP = 64
SLOTS = 4
TOK_DEV = 1024
OWNERS = 32
KEYS = 512
VALS = 1024
TOKENS = 32768


def draw_lengths(key, part):
    key = jax.random.fold_in(key, 11)
    per_device = TOK_DEV // GROUP
    key_totals, key_cuts, key_full = jax.random.split(key, 3)
    totals = jax.random.randint(key_totals, (OWNERS,), per_device // 2, per_device + 1, dtype=jnp.int32)
    cuts = jax.random.randint(key_cuts, (OWNERS, SLOTS - 1), 0, totals[:, None] + 1, dtype=jnp.int32)
    cuts = jnp.sort(cuts, axis=1).astype(jnp.int32)
    edges = jnp.concatenate([jnp.zeros((OWNERS, 1), jnp.int32), cuts, totals[:, None].astype(jnp.int32)], axis=1)
    counts = (edges[:, 1:] - edges[:, :-1]).astype(jnp.int32)
    full_device = jax.random.randint(key_full, (), 0, OWNERS, dtype=jnp.int32)
    single = jnp.zeros((SLOTS,), jnp.int32).at[0].set(per_device)
    chosen = (jnp.arange(OWNERS, dtype=jnp.int32) == full_device)[:, None]
    counts = jnp.where(chosen, single[None, :], counts)
    return (counts * GROUP).astype(jnp.int32)


def block_levels(stream_key, shape, pieces, least, top_value):
    def one(position, shards_of):
        draws = jax.random.uniform(jax.random.fold_in(jax.random.fold_in(stream_key, 6), position), (shards_of,), jnp.float32, least / len(pieces), top_value / len(pieces))
        return jnp.repeat(jnp.exp(draws), shape[position] // shards_of).reshape((-1,) + (1,) * (len(shape) - position - 1))

    loudness = one(*pieces[0])
    for cut in pieces[1:]:
        loudness = loudness * one(*cut)
    return loudness


def bell_draw(stream_key, dims, scale, most, shards=(), held_as=jnp.bfloat16):
    entries = scale * jax.random.normal(stream_key, dims, jnp.float32)
    if shards:
        entries = entries * block_levels(stream_key, dims, shards, -0.22, 0.18)
    return jnp.clip(entries, -most, most).astype(held_as)


def setup_inputs(seed: int = 0) -> dict:
    keys = jax.random.split(jax.random.key(seed), 18)
    tokens = bell_draw(keys[0], (TOKENS, D), 1.0, 6.0, ((0, 32),))
    cotangent = bell_draw(keys[1], (TOKENS, D), 1.0, 6.0, ((0, 32),))
    lengths = draw_lengths(jax.random.fold_in(keys[17], 71), 0)
    attn_gain = jnp.clip(1.0 + 0.1 * jax.random.normal(keys[3], (D,), jnp.float32), 0.5, 1.5).astype(jnp.bfloat16)
    w_query = bell_draw(keys[4], (D, KEYS), D ** -0.5, 0.1875, ((0, 32),))
    w_key = bell_draw(keys[5], (D, KEYS), D ** -0.5, 0.1875, ((0, 32),))
    w_value = bell_draw(keys[6], (D, VALS), D ** -0.5, 0.1875, ((0, 32),))
    w_outgate = bell_draw(keys[7], (D, VALS), D ** -0.5, 0.1875, ((0, 32),))
    w_down_rank = bell_draw(keys[8], (D, RANK), D ** -0.5, 0.1875, ((0, 32),))
    w_up_rank = bell_draw(keys[9], (RANK, KEYS), RANK ** -0.5, 1.5, ((1, 32),))
    rank_bias = jnp.clip(0.5 + 4.5 * jax.random.uniform(keys[10], (KEYS,), jnp.float32) ** block_levels(keys[10], (KEYS,), ((0, 32),), -0.2, 0.2), 0.5, 5.0).astype(jnp.bfloat16)
    head_gain = jnp.clip(1.0 + 0.1 * jax.random.normal(keys[11], (DV,), jnp.float32), 0.5, 1.5).astype(jnp.bfloat16)
    w_output = bell_draw(keys[12], (VALS, D), (VALS // 4) ** -0.5, 0.375, ((0, 32),))
    ffn_gain = jnp.clip(1.0 + 0.1 * jax.random.normal(keys[13], (D,), jnp.float32), 0.5, 1.5).astype(jnp.bfloat16)
    w_ffn_gate = bell_draw(keys[14], (D, FF), D ** -0.5, 0.1875, ((0, 32),))
    w_ffn_up = bell_draw(keys[15], (D, FF), D ** -0.5, 0.1875, ((0, 32),))
    w_ffn_down = bell_draw(keys[16], (FF, D), (FF // 4) ** -0.5, 0.21875, ((0, 32),))
    return dict(tokens=tokens, cotangent=cotangent, lengths=lengths, attn_gain=attn_gain, w_query=w_query, w_key=w_key, w_value=w_value, w_outgate=w_outgate, w_down_rank=w_down_rank, w_up_rank=w_up_rank, rank_bias=rank_bias, head_gain=head_gain, w_output=w_output, ffn_gain=ffn_gain, w_ffn_gate=w_ffn_gate, w_ffn_up=w_ffn_up, w_ffn_down=w_ffn_down)


EPS = 1e-05
HEAD_EPS = 0.1
precise = lax.Precision.HIGHEST

@jax.custom_vjp
def low(v):
    return lax.optimization_barrier(v.astype(jnp.bfloat16)).astype(jnp.float32)

@jax.custom_vjp
def low_back(v):
    return v

def low_keep(v):
    return (low(v), None)

def low_pass(kept, grad):
    return (grad,)

def back_keep(v):
    return (v, None)

def back_low(kept, grad):
    return (low(grad),)
low.defvjp(low_keep, low_pass)
low_back.defvjp(back_keep, back_low)

def layout(length_row, slot_count, block_len):
    row_ints = length_row.astype(jnp.int32)
    ends = jnp.cumsum(row_ints, dtype=jnp.int32).astype(jnp.int32)
    starts = jnp.concatenate([(ends - row_ints).astype(jnp.int32), ends[-1:].astype(jnp.int32)])
    begins = jnp.arange(slot_count // block_len, dtype=jnp.int32) * block_len
    restart = jnp.any(begins[:, None] == starts[None, :], axis=1).astype(jnp.float32)
    valid = (jnp.arange(slot_count, dtype=jnp.int32) < ends[-1]).astype(jnp.float32)
    return (restart, valid)

def rms_norm(values, gain, floor_eps=EPS):
    return values * lax.rsqrt(lax.optimization_barrier(jnp.mean(values * values, axis=-1, keepdims=True)) + floor_eps) * gain

def matmul(left, right):
    return jnp.dot(left, right, precision=precise)

def mixer_core(queries, key_rows, val_rows, decay_logit, gate_rows, head_gain, restart):
    blocks = restart.shape[0]
    width = queries.shape[0] // blocks
    decay = jax.nn.log_sigmoid(decay_logit) / 16.0
    scaled = (queries * DK ** (-0.5)).reshape(blocks, width, HEADS, DK)
    keyed = key_rows.reshape(blocks, width, HEADS, DK)
    valued = val_rows.reshape(blocks, width, HEADS, DV)
    cumulative = jnp.cumsum(decay.reshape(blocks, width, HEADS, DK), axis=1)
    block_total = cumulative[:, -1]
    q_read = scaled * jnp.exp(cumulative)
    k_read = keyed * jnp.exp(-cumulative)
    k_write = keyed * jnp.exp(block_total[:, None] - cumulative)
    causal = jnp.tril(jnp.ones((width, width), queries.dtype))
    scores = jnp.einsum('nthc,nshc->nhts', q_read, k_read, precision=precise) * causal
    within = jnp.einsum('nhts,nshv->nthv', scores, valued, precision=precise)
    updates = jnp.einsum('nshc,nshv->nhcv', k_write, valued, precision=precise)
    reset_rows = restart.astype(updates.dtype)

    def advance(carried, inputs_now):
        update_now, total_now, reset_now = inputs_now
        kept = carried * (1.0 - reset_now)
        return (kept * jnp.exp(total_now)[:, :, None] + update_now, kept)
    start_state = jnp.zeros((HEADS, DK, DV), updates.dtype)
    _, before = lax.scan(advance, start_state, (updates, block_total, reset_rows))
    across = jnp.einsum('nthc,nhcv->nthv', q_read, before, precision=precise)
    combined = within + across
    normed = rms_norm(combined, head_gain, HEAD_EPS)
    gates = gate_rows.reshape(blocks, width, HEADS, DV)
    return (normed * jax.nn.silu(gates)).reshape(blocks * width, HEADS * DV)

def block_forward(source, params, restart, valid):
    attn_gain, w_query, w_key, w_value, w_outgate, w_down_rank, w_up_rank, rank_bias, head_gain, w_output, ffn_gain, w_ffn_gate, w_ffn_up, w_ffn_down = params
    normed_in = low(rms_norm(source, attn_gain))
    queries = low_back(matmul(normed_in, w_query))
    key_rows = low_back(matmul(normed_in, w_key))
    val_rows = low_back(matmul(normed_in, w_value))
    gate_rows = low_back(matmul(normed_in, w_outgate))
    low_rank = low(low_back(matmul(normed_in, w_down_rank)))
    decay_logit = low_back(matmul(low_rank, w_up_rank)) + rank_bias
    head_out = low(mixer_core(queries, key_rows, val_rows, decay_logit, gate_rows, head_gain, restart))
    middle = source + low_back(matmul(head_out, w_output))
    normed_mid = low(rms_norm(middle, ffn_gain))
    ffn_pre = low_back(matmul(normed_mid, w_ffn_gate))
    ffn_lin = low_back(matmul(normed_mid, w_ffn_up))
    hidden = low(jax.nn.silu(ffn_pre) * ffn_lin)
    result = middle + low_back(matmul(hidden, w_ffn_down))
    return result * valid[:, None]

def reference(tokens, cotangent, lengths, attn_gain, w_query, w_key, w_value, w_outgate, w_down_rank, w_up_rank, rank_bias, head_gain, w_output, ffn_gain, w_ffn_gate, w_ffn_up, w_ffn_down):
    params = tuple((weight.astype(jnp.float32) for weight in (attn_gain, w_query, w_key, w_value, w_outgate, w_down_rank, w_up_rank, rank_bias, head_gain, w_output, ffn_gain, w_ffn_gate, w_ffn_up, w_ffn_down)))
    source_all = tokens.astype(jnp.float32).reshape(OWNERS, TOK_DEV, D)
    upstream_all = cotangent.astype(jnp.float32).reshape(OWNERS, TOK_DEV, D)
    length_all = lengths.astype(jnp.int32)

    def visit(summed, inputs_now):
        source, upstream, length_row = inputs_now
        restart, valid = layout(length_row, TOK_DEV, GROUP)
        restart = restart.astype(source.dtype)
        valid = valid.astype(source.dtype)

        def forward(source_in, params_in):
            return block_forward(source_in, params_in, restart, valid)
        result, pullback = jax.vjp(forward, source, params)
        source_grad, param_grads = pullback(upstream)
        summed = tuple((left + right.astype(left.dtype) for left, right in zip(summed, param_grads)))
        return (summed, (result.astype(jnp.bfloat16), source_grad.astype(jnp.bfloat16)))
    start_sums = tuple((jnp.zeros_like(weight) for weight in params))
    grads, (results, source_grads) = lax.scan(visit, start_sums, (source_all, upstream_all, length_all))
    return (results.reshape(TOKENS, D), source_grads.reshape(TOKENS, D), grads[0], grads[1], grads[2], grads[3], grads[4], grads[5], grads[6], grads[7], grads[8], grads[9], grads[10], grads[11], grads[12], grads[13])
```

```python
import jax
import jax.numpy as jnp
from jax import lax
from jax.sharding import PartitionSpec as P

HEADS = 4
DK = 128
DV = 256
GROUP = 64


EPS = 1e-05
HEAD_EPS = 0.1
precise = lax.Precision.HIGH


def layout(length_row, slot_count, block_len):
    ends = jnp.cumsum(length_row, dtype=jnp.int32)
    starts = jnp.concatenate([ends - length_row, ends[-1:]])
    begins = jnp.arange(slot_count // block_len, dtype=jnp.int32) * block_len
    restart = jnp.any(begins[:, None] == starts[None, :], axis=1).astype(jnp.float32)
    valid = (jnp.arange(slot_count, dtype=jnp.int32) < ends[-1]).astype(jnp.float32)
    return (restart, valid)


def rms_norm(values, gain, floor_eps=EPS):
    return values * lax.rsqrt(jnp.mean(values * values, axis=-1, keepdims=True) + floor_eps) * gain


def mixer_core(queries, key_rows, val_rows, decay_logit, gate_rows, head_gain, restart):
    blocks = restart.shape[0]
    width = queries.shape[0] // blocks
    decay = jax.nn.log_sigmoid(decay_logit) / 16.0
    scaled = (queries * DK ** (-0.5)).reshape(blocks, width, HEADS, DK)
    keyed = key_rows.reshape(blocks, width, HEADS, DK)
    valued = val_rows.reshape(blocks, width, HEADS, DV)
    cumulative = jnp.cumsum(decay.reshape(blocks, width, HEADS, DK), axis=1)
    block_total = cumulative[:, -1]
    q_read = scaled * jnp.exp(cumulative)
    k_read = keyed * jnp.exp(-cumulative)
    k_write = keyed * jnp.exp(block_total[:, None] - cumulative)
    causal = jnp.tril(jnp.ones((width, width), jnp.float32))
    scores = jnp.einsum("nthc,nshc->nhts", q_read, k_read, precision=precise) * causal
    within = jnp.einsum("nhts,nshv->nthv", scores, valued, precision=precise)
    updates = jnp.einsum("nshc,nshv->nhcv", k_write, valued, precision=precise)

    def advance(carried, inputs_now):
        update_now, total_now, reset_now = inputs_now
        kept = carried * (1.0 - reset_now)
        return (kept * jnp.exp(total_now)[:, :, None] + update_now, kept)

    start_state = jnp.zeros((HEADS, DK, DV), jnp.float32)
    _, before = lax.scan(advance, start_state, (updates, block_total, restart), unroll=True)
    across = jnp.einsum("nthc,nhcv->nthv", q_read, before, precision=precise)
    combined = within + across
    normed = rms_norm(combined, head_gain, HEAD_EPS)
    gates = gate_rows.reshape(blocks, width, HEADS, DV)
    return (normed * jax.nn.silu(gates)).reshape(blocks * width, HEADS * DV)


def swish_product(pre_rows, lin_rows):
    return jax.nn.silu(pre_rows) * lin_rows


def linear(left, right):
    return jnp.dot(left, right, preferred_element_type=jnp.float32)


def linear_tn(left, right):
    return lax.dot_general(
        left, right, (((0,), (0,)), ((), ())), preferred_element_type=jnp.float32
    )


def linear_nt(left, right):
    return lax.dot_general(
        left, right, (((1,), (1,)), ((), ())), preferred_element_type=jnp.float32
    )


AXES = ("dp", "fsdp")
SMALL = 128


def gather(shard):
    return lax.all_gather(shard, AXES, axis=0, tiled=True)


def scatter(term):
    return lax.psum_scatter(term, AXES, scatter_dimension=0, tiled=True)


def pack_small(parts, rows):
    flat = jnp.concatenate(parts, axis=1)
    owners, width = flat.shape
    flat = jnp.pad(flat, ((0, 0), (0, rows * SMALL - width)))
    return flat.reshape(owners * rows, SMALL)


def unpack_small(block, owners, widths):
    flat = block.reshape(owners, -1)
    parts, at = [], 0
    for width in widths:
        parts.append(flat[:, at : at + width])
        at += width
    return parts


def local(
    tokens,
    cotangent,
    lengths,
    attn_gain,
    w_query,
    w_key,
    w_value,
    w_outgate,
    w_down_rank,
    w_up_rank,
    rank_bias,
    head_gain,
    w_output,
    ffn_gain,
    w_ffn_gate,
    w_ffn_up,
    w_ffn_down,
):
    rows, keys = w_query.shape
    model = tokens.shape[1]
    owners = model // rows
    vals = w_value.shape[1]
    rank = w_down_rank.shape[1]
    inner = w_ffn_gate.shape[1]
    wide = 2 * keys + 2 * vals
    shards = (w_down_rank, attn_gain, w_up_rank, rank_bias, head_gain, ffn_gain)
    widths = [shard.size for shard in shards]
    small_shard = jnp.concatenate([shard.reshape(-1) for shard in shards])
    small_shard = jnp.pad(small_shard, (0, rows * SMALL - sum(widths))).reshape(rows, SMALL)
    mixer = gather(
        jnp.concatenate([w_query, w_key, w_value, w_outgate, w_output, small_shard], axis=1)
    )
    full_gate_up = gather(jnp.concatenate([w_ffn_gate, w_ffn_up], axis=1))
    full_ffn_down = gather(w_ffn_down)
    full_in = mixer[:, :wide]
    full_output = mixer[:, wide : wide + model]
    small = unpack_small(mixer[:, wide + model :], owners, widths)
    full_down_rank = small[0].reshape(model, rank)
    full_gain = small[1].reshape(-1)
    full_up_rank = small[2].reshape(owners, rank, -1).transpose(1, 0, 2).reshape(rank, keys)
    full_bias = small[3].reshape(-1)
    full_head_gain = small[4].reshape(-1)
    ffn_full_gain = small[5].reshape(-1)
    restart, valid = layout(lengths[0], tokens.shape[0], GROUP)
    source = tokens.astype(jnp.float32)
    normed_f, norm_in_pull = jax.vjp(rms_norm, source, full_gain.astype(jnp.float32))
    normed_in = normed_f.astype(jnp.bfloat16)
    projected = linear(normed_in, full_in)
    queries = projected[:, :keys]
    key_rows = projected[:, keys : 2 * keys]
    val_rows = projected[:, 2 * keys : 2 * keys + vals]
    gate_rows = projected[:, 2 * keys + vals :]
    low_rank = linear(normed_in, full_down_rank).astype(jnp.bfloat16)
    decay_logit = linear(low_rank, full_up_rank) + full_bias.astype(jnp.float32)

    def core_of(query_in, key_in, value_in, logit_in, gate_in, gain_in):
        return mixer_core(query_in, key_in, value_in, logit_in, gate_in, gain_in, restart)

    core_out, core_pull = jax.vjp(
        core_of,
        queries,
        key_rows,
        val_rows,
        decay_logit,
        gate_rows,
        full_head_gain.astype(jnp.float32),
    )
    head_out = core_out.astype(jnp.bfloat16)
    middle = source + linear(head_out, full_output)
    normed_mid_f, norm_mid_pull = jax.vjp(rms_norm, middle, ffn_full_gain.astype(jnp.float32))
    normed_mid = normed_mid_f.astype(jnp.bfloat16)
    ffn_both = linear(normed_mid, full_gate_up)
    ffn_pre = ffn_both[:, :inner]
    ffn_lin = ffn_both[:, inner:]
    hidden_f, hidden_pull = jax.vjp(swish_product, ffn_pre, ffn_lin)
    hidden = hidden_f.astype(jnp.bfloat16)
    mixed = ((middle + linear(hidden, full_ffn_down)) * valid[:, None]).astype(jnp.bfloat16)
    upstream = cotangent.astype(jnp.float32) * valid[:, None]
    g_out = upstream.astype(jnp.bfloat16)
    grad_ffn_down = linear_tn(hidden, g_out)
    g_hidden = linear_nt(g_out, full_ffn_down)
    g_pre_f, g_lin_f = hidden_pull(g_hidden)
    g_both = jnp.concatenate([g_pre_f, g_lin_f], axis=1).astype(jnp.bfloat16)
    grad_gate_up = linear_tn(normed_mid, g_both)
    g_norm_mid = linear_nt(g_both, full_gate_up)
    g_mid_norm, grad_ffn_gain = norm_mid_pull(g_norm_mid)
    g_middle = upstream + g_mid_norm
    g_mix = g_middle.astype(jnp.bfloat16)
    grad_output = linear_tn(head_out, g_mix)
    g_mix, grad_ffn_down, grad_gate_up = lax.optimization_barrier(
        (g_mix, grad_ffn_down, grad_gate_up)
    )
    down_part = scatter(grad_ffn_down)
    gate_up_part = scatter(grad_gate_up)
    g_head = linear_nt(g_mix, full_output)
    g_queries_f, g_keys_f, g_vals_f, g_logit, g_gates_f, grad_head_gain = core_pull(g_head)
    g_in = jnp.concatenate([g_queries_f, g_keys_f, g_vals_f, g_gates_f], axis=1).astype(
        jnp.bfloat16
    )
    g_low = g_logit.astype(jnp.bfloat16)
    grad_rank_bias = jnp.sum(g_logit, axis=0)
    grad_up_rank = linear_tn(low_rank, g_low)
    g_rank = linear_nt(g_low, full_up_rank).astype(jnp.bfloat16)
    grad_down_rank = linear_tn(normed_in, g_rank)
    grad_in = linear_tn(normed_in, g_in)
    g_norm_in = linear_nt(g_in, full_in) + linear_nt(g_rank, full_down_rank)
    g_source_norm, grad_attn_gain = norm_in_pull(g_norm_in)
    token_grad = (g_middle + g_source_norm).astype(jnp.bfloat16)
    terms = (
        grad_down_rank,
        grad_attn_gain,
        grad_up_rank.reshape(rank, owners, -1).transpose(1, 0, 2),
        grad_rank_bias,
        grad_head_gain,
        grad_ffn_gain,
    )
    small_terms = pack_small([term.reshape(owners, -1) for term in terms], rows)
    part = scatter(jnp.concatenate([grad_in, grad_output, small_terms], axis=1))
    small_part = unpack_small(part[:, wide + model :], 1, widths)
    return (
        mixed,
        token_grad,
        small_part[1].reshape(-1),
        part[:, :keys],
        part[:, keys : 2 * keys],
        part[:, 2 * keys : 2 * keys + vals],
        part[:, 2 * keys + vals : wide],
        small_part[0].reshape(rows, rank),
        small_part[2].reshape(rank, -1),
        small_part[3].reshape(-1),
        small_part[4].reshape(-1),
        part[:, wide : wide + model],
        small_part[5].reshape(-1),
        gate_up_part[:, :inner],
        gate_up_part[:, inner:],
        down_part,
    )


def solution(mesh):
    return jax.shard_map(
        local,
        mesh=mesh,
        in_specs=(
            P(("dp", "fsdp"), None),
            P(("dp", "fsdp"), None),
            P(("dp", "fsdp"), None),
            P(("dp", "fsdp")),
            P(("dp", "fsdp"), None),
            P(("dp", "fsdp"), None),
            P(("dp", "fsdp"), None),
            P(("dp", "fsdp"), None),
            P(("dp", "fsdp"), None),
            P(None, ("dp", "fsdp")),
            P(("dp", "fsdp")),
            P(("dp", "fsdp")),
            P(("dp", "fsdp"), None),
            P(("dp", "fsdp")),
            P(("dp", "fsdp"), None),
            P(("dp", "fsdp"), None),
            P(("dp", "fsdp"), None),
        ),
        out_specs=(
            P(("dp", "fsdp"), None),
            P(("dp", "fsdp"), None),
            P(("dp", "fsdp")),
            P(("dp", "fsdp"), None),
            P(("dp", "fsdp"), None),
            P(("dp", "fsdp"), None),
            P(("dp", "fsdp"), None),
            P(("dp", "fsdp"), None),
            P(None, ("dp", "fsdp")),
            P(("dp", "fsdp")),
            P(("dp", "fsdp")),
            P(("dp", "fsdp"), None),
            P(("dp", "fsdp")),
            P(("dp", "fsdp"), None),
            P(("dp", "fsdp"), None),
            P(("dp", "fsdp"), None),
        ),
        check_vma=False,
    )
```
